512 devices in a mesh: dp: 16 (over z_hi, y, core), tensor: 32 (over x, z_lo).
Axes of the slice: x: 4, y: 4, z: 16 (z_hi: 2, z_lo: 8; z = z_hi * 8 + z_lo), core: 2. Of those that a mesh axis runs over, the one named last changes fastest.
Arguments:
- tokens: bfloat16 [128, 16, 4096], P(None, 'dp', 'tensor'), may hold values from -6 to 6
- gate_weight: bfloat16 [4096, 14336], P('dp', 'tensor'), may hold values from -0.09375 to 0.09375
- up_weight: bfloat16 [4096, 14336], P('dp', 'tensor'), may hold values from -0.09375 to 0.09375
- down_weight: bfloat16 [14336, 4096], P('tensor', 'dp'), may hold values from -0.046875 to 0.046875
- ia3_scale: float32 [14336], P('tensor'), may hold values from 0.3 to 3
- cotangent: bfloat16 [128, 16, 4096], P(None, 'dp', 'tensor'), may hold values from -4 to 4
Outputs:
- mixed: bfloat16 [128, 16, 4096], P(None, 'dp', 'tensor')
- input_grad: bfloat16 [128, 16, 4096], P(None, 'dp', 'tensor')
- scale_grad: float32 [14336], P('tensor')
The draws below stay inside these ranges and needn't reach their ends.
All inputs are finite; a program needn't handle non-finite values.
Results may differ from the reference program's by a relative error of at most 0.0049.
Values may be sent and summed in bfloat16 or wider, within the bound.
No kernel may reach another device: no remote copies, remote signals or barrier semaphores. Data moves between devices by JAX's collectives and lax.ppermute only.
A program may use at most 64 MiB of HBM per device.

```python
import math
import jax
import jax.numpy as jnp
from jax import lax

D = 4096
FF = 14336
LEN = 128
SEQS = 16


def shard_levels(own_key, extent, cuts, least, top_value):
    gain = 1.0
    for dim, parts in cuts:
        heights = jax.random.uniform(jax.random.fold_in(jax.random.fold_in(own_key, 6), dim), (parts,), jnp.float32, least / len(cuts), top_value / len(cuts))
        gain = gain * jnp.repeat(jnp.exp(heights), extent[dim] // parts).reshape((-1,) + (1,) * (len(extent) - 1 - dim))
    return gain


def centred(own_key, dims, deviation, most, shards=(), held_as=jnp.bfloat16):
    values = deviation * jax.random.normal(own_key, dims, jnp.float32)
    if shards:
        values = values * shard_levels(own_key, dims, shards, -0.22, 0.18)
    return jnp.clip(values, -most, most).astype(held_as)


def setup_inputs(seed: int = 0) -> dict:
    key_of = jax.random.split(jax.random.key(seed), 7)
    tokens = centred(key_of[0], (LEN, SEQS, D), 1.0, 6.0, ((1, 16), (2, 32)))
    gate_weight = centred(key_of[1], (D, FF), D ** -0.5, 0.09375, ((0, 16), (1, 32)))
    up_weight = centred(key_of[2], (D, FF), D ** -0.5, 0.09375, ((0, 16), (1, 32)))
    down_weight = centred(key_of[3], (FF, D), FF ** -0.5, 0.046875, ((0, 32), (1, 16)))
    ia3_scale = jnp.clip(jnp.exp(math.log(3.0) - 2.3025851 * jax.random.uniform(key_of[4], (FF,), jnp.float32) ** shard_levels(key_of[4], (FF,), ((0, 32),), -0.2, 0.2)), 0.3, 3.0)
    cotangent = centred(key_of[5], (LEN, SEQS, D), 0.25, 4.0, ((1, 16), (2, 32)))
    return {"tokens": tokens, "gate_weight": gate_weight, "up_weight": up_weight, "down_weight": down_weight, "ia3_scale": ia3_scale, "cotangent": cotangent}


def reference(tokens, gate_weight, up_weight, down_weight, ia3_scale, cotangent):
    token_rows = tokens.reshape(-1, D)
    grad_rows = cotangent.reshape(-1, D)
    gate_pre = jnp.dot(token_rows, gate_weight, preferred_element_type=jnp.float32)
    up_proj = jnp.dot(token_rows, up_weight, preferred_element_type=jnp.float32)
    sigmoid_gate = jax.nn.sigmoid(gate_pre)
    swish_gate = gate_pre * sigmoid_gate
    activated = swish_gate * up_proj
    hidden = (activated * ia3_scale).astype(jnp.bfloat16)
    mixed = jnp.dot(hidden, down_weight, preferred_element_type=jnp.float32).astype(jnp.bfloat16).reshape(tokens.shape)
    back = lax.dot_general(grad_rows, down_weight, (((1,), (1,)), ((), ())), preferred_element_type=jnp.float32)
    scale_grad = jnp.sum(back * activated, axis=0)
    hidden_grad = back * ia3_scale
    gate_grad = (hidden_grad * up_proj * sigmoid_gate * (1.0 + gate_pre * (1.0 - sigmoid_gate))).astype(jnp.bfloat16)
    up_grad = (hidden_grad * swish_gate).astype(jnp.bfloat16)
    first_term = lax.dot_general(gate_grad, gate_weight, (((1,), (1,)), ((), ())), preferred_element_type=jnp.float32)
    second_term = lax.dot_general(up_grad, up_weight, (((1,), (1,)), ((), ())), preferred_element_type=jnp.float32)
    input_grad = (first_term + second_term).astype(jnp.bfloat16).reshape(tokens.shape)
    return (mixed, input_grad, scale_grad)
```

```python
import jax
import jax.numpy as jnp
from jax import lax
from jax.sharding import Mesh, PartitionSpec as P

ROWS_AXES = ("zh", "y", "c")
COLS_AXES = ("x", "zl")


def spread(block, axis, size):
    copies = jnp.broadcast_to(block[None], (size,) + block.shape)
    return lax.all_to_all(copies, axis, 0, 0, tiled=True)


def swap(block, axis):
    return lax.ppermute(block, axis, [(0, 1), (1, 0)])


def make_per_device(size):
    nh, ny, nc, nx, nl = (size[a] for a in ("zh", "y", "c", "x", "zl"))

    def per_device(tokens, gate_weight, up_weight, down_weight, ia3_scale, cotangent):
        seq_len, seq_local, width = tokens.shape
        rows = seq_len * seq_local
        model = width * nx * nl
        depth = model // (nh * ny * nc)
        hid = gate_weight.shape[1]
        zh, c = lax.axis_index("zh"), lax.axis_index("c")

        def gather(weight):
            other = swap(weight, "zh")
            first = jnp.where(zh == 0, weight, other)
            second = jnp.where(zh == 0, other, weight)
            column = spread(jnp.stack([first, second]), "y", ny)
            return column, swap(column, "c")

        acts = jnp.stack([tokens.reshape(rows, width), cotangent.reshape(rows, width)])
        acts = spread(acts, "zl", nl)
        acts = spread(acts, "x", nx)
        acts = acts.transpose(2, 3, 0, 1, 4).reshape(2, rows, nh, ny, nc, depth)
        acts = acts.transpose(0, 4, 1, 3, 2, 5).reshape(2, nc, rows, model // nc)
        tok = [lax.dynamic_index_in_dim(acts[0], k, 0, False) for k in (c, 1 - c)]
        cot = [lax.dynamic_index_in_dim(acts[1], k, 0, False) for k in (c, 1 - c)]

        gate = [w.reshape(-1, hid) for w in gather(gate_weight)]
        up = [w.reshape(-1, hid) for w in gather(up_weight)]
        down = [w.reshape(-1, hid) for w in gather(down_weight.T)]

        def times(a, b):
            parts = [jnp.dot(p, q, preferred_element_type=jnp.float32) for p, q in zip(a, b)]
            return parts[0] + parts[1]

        gate_pre = times(tok, gate)
        up_proj = times(tok, up)
        back = times(cot, down)
        sigmoid_gate = jax.nn.sigmoid(gate_pre)
        swish_gate = gate_pre * sigmoid_gate
        activated = swish_gate * up_proj
        hidden = (activated * ia3_scale).astype(jnp.bfloat16)
        local_grad = jnp.sum(back * activated, axis=0)
        hidden_grad = back * ia3_scale
        gate_grad = (
            hidden_grad * up_proj * sigmoid_gate * (1.0 + gate_pre * (1.0 - sigmoid_gate))
        ).astype(jnp.bfloat16)
        up_grad = (hidden_grad * swish_gate).astype(jnp.bfloat16)

        def turned(a, b):
            return lax.dot_general(
                a, b, (((1,), (1,)), ((), ())), preferred_element_type=jnp.float32
            )

        def partial(k):
            mixed = turned(hidden, down[k])
            grad = turned(gate_grad, gate[k]) + turned(up_grad, up[k])
            return jnp.stack([mixed, grad]).astype(jnp.bfloat16)

        own, other = partial(0), partial(1)
        first = jnp.where(c == 0, own, other)
        second = jnp.where(c == 0, other, own)
        outs = jnp.stack([first, second])
        outs = outs.reshape(nc, 2, rows, ny, nh, depth).transpose(4, 3, 0, 5, 1, 2)
        outs = outs.reshape(nx, nl, width, 2, rows).transpose(0, 1, 3, 4, 2)
        outs = lax.all_to_all(outs, "x", 0, 0, tiled=True)
        outs = jnp.sum(outs.astype(jnp.float32), axis=0).astype(jnp.bfloat16)
        outs = lax.all_to_all(outs, "zl", 0, 0, tiled=True)
        outs = jnp.sum(outs.astype(jnp.float32), axis=0).astype(jnp.bfloat16)
        mixed = outs[0].reshape(tokens.shape)
        input_grad = outs[1].reshape(tokens.shape)
        scale_grad = jnp.sum(spread(local_grad, ROWS_AXES, nh * ny * nc), axis=0)
        return mixed, input_grad, scale_grad

    return per_device


def solution(mesh):
    shape = {"zh": 2, "y": 4, "c": 2, "x": 4, "zl": 8}
    fine = Mesh(mesh.devices.reshape(tuple(shape.values())), tuple(shape))
    in_specs = (
        P(None, ROWS_AXES, COLS_AXES),
        P(ROWS_AXES, COLS_AXES),
        P(ROWS_AXES, COLS_AXES),
        P(COLS_AXES, ROWS_AXES),
        P(COLS_AXES),
        P(None, ROWS_AXES, COLS_AXES),
    )
    out_specs = (
        P(None, ROWS_AXES, COLS_AXES),
        P(None, ROWS_AXES, COLS_AXES),
        P(COLS_AXES),
    )
    return jax.shard_map(
        make_per_device(shape),
        mesh=fine,
        in_specs=in_specs,
        out_specs=out_specs,
        check_vma=False,
    )
```

```python
import jax
import jax.numpy as jnp
from jax import lax
from jax.experimental import pallas as pl
from jax.experimental.pallas import tpu as pltpu
from jax.sharding import Mesh, PartitionSpec as P

ROWS_AXES = ("zh", "y", "c")
COLS_AXES = ("x", "zl")
F32 = jnp.float32
BF16 = jnp.bfloat16


def spread(block, axis, size):
    copies = jnp.broadcast_to(block[None], (size,) + block.shape)
    return lax.all_to_all(copies, axis, 0, 0, tiled=True)


def shifted(block, axis, size):
    return [block] + [
        lax.ppermute(block, axis, [(i, (i + n) % size) for i in range(size)])
        for n in range(1, size)
    ]


def swap(block, axis):
    return lax.ppermute(block, axis, [(0, 1), (1, 0)])


def fetch(place, pairs, weights, sems):
    copies = []
    for pair in pairs:
        ny, matrices, _, depth = pair[0].shape
        for m in range(matrices):
            row = []
            for k, ref in enumerate(pair):
                core = jnp.bitwise_xor(place[1], k)
                for y in range(ny):
                    at = pl.multiple_of((y * 2 + core) * depth, depth)
                    copy = pltpu.make_async_copy(
                        ref.at[y, m],
                        weights.at[len(copies), :, pl.ds(at, depth)],
                        sems.at[len(copies), k * ny + y],
                    )
                    copy.start()
                    row.append(copy)
            copies.append(row)
    return copies


def near_kernel(
    place,
    acts_0, acts_1, acts_2, acts_3,
    own, core,
    part,
    tok_far,
    tok,
    weights,
    sems,
):
    acts = (acts_0, acts_1, acts_2, acts_3)
    nx = len(acts)
    nl, _, rows, width = acts_0.shape
    zh, me = place[0], place[2]
    copies = fetch(place, [(own, core)], weights, sems)

    for n in range(nx):
        x = lax.rem(me - n + nx, nx)
        base = lax.rem(x, nx // 2) * (nl * width)
        far = jnp.bitwise_xor(x // (nx // 2), zh)
        for zl in range(nl):
            at = pl.multiple_of(base + zl * width, width)
            for t in range(2):
                tok[far, t, :, pl.ds(at, width)] = acts[n][zl, t]
    tok_far[...] = tok[1]

    for m in range(3):
        for copy in copies[m]:
            copy.wait()
        part[m] = lax.dot_general(
            tok[0, m // 2], weights[m], (((1,), (1,)), ((), ())), preferred_element_type=F32
        )


def layer_kernel(
    place,
    part,
    tok_far,
    scale,
    near_own, near_core,
    first_own, first_core, last_own, last_core,
    outs,
    grad,
    near,
    far,
    sems,
):
    nx, nl, _, rows, width = outs.shape
    zh = place[0]
    far_copies = fetch(place, [(first_own, first_core), (last_own, last_core)], far, sems.at[1])
    near_copies = fetch(place, [(near_own, near_core)], near, sems.at[0])

    def times(t, m):
        for copy in far_copies[m]:
            copy.wait()
        return part[m] + lax.dot_general(
            tok_far[t], far[m], (((1,), (1,)), ((), ())), preferred_element_type=F32
        )

    gate_pre = times(0, 0)
    up_proj = times(0, 1)
    back = times(1, 2)
    sigmoid_gate = jax.nn.sigmoid(gate_pre)
    swish_gate = gate_pre * sigmoid_gate
    activated = swish_gate * up_proj
    hidden = (activated * scale[...]).astype(BF16)
    grad[...] = jnp.sum(back * activated, axis=0, keepdims=True)
    hidden_grad = back * scale[...]
    gate_grad = (
        hidden_grad * up_proj * sigmoid_gate * (1.0 + gate_pre * (1.0 - sigmoid_gate))
    ).astype(BF16)
    up_grad = (hidden_grad * swish_gate).astype(BF16)

    for m in range(3):
        for copy in near_copies[m]:
            copy.wait()
    for k, weights in enumerate((far, near)):
        half = jnp.bitwise_xor(zh, 1 - k)
        for n in range(nx * nl // 4):
            columns = slice(2 * n * width, 2 * (n + 1) * width)
            mixed = jnp.dot(hidden, weights[2, :, columns], preferred_element_type=F32)
            back_in = jnp.dot(
                gate_grad, weights[0, :, columns], preferred_element_type=F32
            ) + jnp.dot(up_grad, weights[1, :, columns], preferred_element_type=F32)
            for side in range(2):
                x, zl = divmod(2 * n + side, nl)
                x = half * (nx // 2) + x
                piece = slice(side * width, (side + 1) * width)
                outs[x, zl, 0] = mixed[:, piece].astype(BF16)
                outs[x, zl, 1] = back_in[:, piece].astype(BF16)


def whole():
    return pl.BlockSpec(memory_space=pltpu.VMEM)


def anywhere():
    return pl.BlockSpec(memory_space=pl.ANY)


def near_layer(place, acts, weights):
    nx = len(acts)
    nl, _, rows, width = acts[0].shape
    ny, _, hid, depth = weights[0].shape
    half = nx * nl * width // 2
    return pl.pallas_call(
        near_kernel,
        out_shape=(
            jax.ShapeDtypeStruct((3, rows, hid), F32),
            jax.ShapeDtypeStruct((2, rows, half), BF16),
        ),
        in_specs=[pl.BlockSpec(memory_space=pltpu.SMEM)] + [whole()] * nx + [anywhere()] * 2,
        out_specs=(whole(), whole()),
        scratch_shapes=[
            pltpu.VMEM((2, 2, rows, half), BF16),
            pltpu.VMEM((3, hid, half), BF16),
            pltpu.SemaphoreType.DMA((3, 2 * ny)),
        ],
        compiler_params=pltpu.CompilerParams(vmem_limit_bytes=48 * 2**20),
        cost_estimate=pl.CostEstimate(
            flops=6 * rows * half * hid, bytes_accessed=6 * half * hid, transcendentals=0
        ),
    )(place, *acts, *weights)


def layer(place, part, tok_far, scale, weights, nx, nl):
    _, rows, half = tok_far.shape
    ny, _, hid, depth = weights[0].shape
    width = 2 * half // (nx * nl)
    return pl.pallas_call(
        layer_kernel,
        out_shape=(
            jax.ShapeDtypeStruct((nx, nl, 2, rows, width), BF16),
            jax.ShapeDtypeStruct((1, hid), F32),
        ),
        in_specs=[pl.BlockSpec(memory_space=pltpu.SMEM)] + [whole()] * 3 + [anywhere()] * 6,
        out_specs=(whole(), whole()),
        scratch_shapes=[
            pltpu.VMEM((3, hid, half), BF16),
            pltpu.VMEM((3, hid, half), BF16),
            pltpu.SemaphoreType.DMA((2, 3, 2 * ny)),
        ],
        compiler_params=pltpu.CompilerParams(vmem_limit_bytes=48 * 2**20),
        cost_estimate=pl.CostEstimate(
            flops=18 * rows * half * hid,
            bytes_accessed=12 * half * hid,
            transcendentals=rows * hid,
        ),
    )(place, part, tok_far, scale, *weights)


def total(blocks):
    wide = [block.astype(F32) for block in blocks]
    while len(wide) > 1:
        wide = [a + b for a, b in zip(wide[::2], wide[1::2])]
    return wide[0]


def make_per_device(size):
    ny, nx, nl = (size[a] for a in ("y", "x", "zl"))

    def per_device(tokens, gate_weight, up_weight, down_weight, ia3_scale, cotangent):
        seq_len, seq_local, width = tokens.shape
        rows = seq_len * seq_local
        place = jnp.stack([lax.axis_index(a) for a in ("zh", "c", "x")])

        acts = jnp.stack([tokens.reshape(rows, width), cotangent.reshape(rows, width)])
        acts = spread(acts, "zl", nl)

        mine = [gate_weight.T, up_weight.T, down_weight]
        mine, acts = lax.optimization_barrier((mine, acts))
        first = [swap(w, "zh") for w in mine[:2]]
        near_own = spread(jnp.stack(mine), "y", ny)
        acts = shifted(acts, "x", nx)
        last = mine[2]
        acts, near_own, first, last = lax.optimization_barrier((acts, near_own, first, last))

        last = swap(last, "zh")
        first_own = spread(jnp.stack(first), "y", ny)
        near_core = swap(near_own, "c")
        part, tok_far = near_layer(place, acts, (near_own, near_core))
        first_own, last, part = lax.optimization_barrier((first_own, last, part))

        first_core = swap(first_own, "c")
        last_own = spread(last[None], "y", ny)
        last_core = swap(last_own, "c")
        weights = (near_own, near_core, first_own, first_core, last_own, last_core)
        outs, grad = layer(place, part, tok_far, ia3_scale.reshape(1, -1), weights, nx, nl)

        grad = grad + swap(grad, "c")
        grad = total(shifted(grad, "y", ny))

        outs = lax.all_to_all(outs, "x", 0, 0, tiled=True)
        outs = total([outs[i] for i in range(nx)]).astype(BF16)
        outs, grad = lax.optimization_barrier((outs, grad))
        scale_grad = (grad + swap(grad, "zh")).reshape(-1)
        outs = lax.all_to_all(outs, "zl", 0, 0, tiled=True)
        outs = total([outs[i] for i in range(nl)]).astype(BF16)
        return outs[0].reshape(tokens.shape), outs[1].reshape(tokens.shape), scale_grad

    return per_device


def solution(mesh):
    shape = {"zh": 2, "y": 4, "c": 2, "x": 4, "zl": 8}
    fine = Mesh(mesh.devices.reshape(tuple(shape.values())), tuple(shape))
    in_specs = (
        P(None, ROWS_AXES, COLS_AXES),
        P(ROWS_AXES, COLS_AXES),
        P(ROWS_AXES, COLS_AXES),
        P(COLS_AXES, ROWS_AXES),
        P(COLS_AXES),
        P(None, ROWS_AXES, COLS_AXES),
    )
    out_specs = (
        P(None, ROWS_AXES, COLS_AXES),
        P(None, ROWS_AXES, COLS_AXES),
        P(COLS_AXES),
    )
    return jax.shard_map(
        make_per_device(shape),
        mesh=fine,
        in_specs=in_specs,
        out_specs=out_specs,
        check_vma=False,
    )
```

```python
import jax
import jax.numpy as jnp
from jax import lax
from jax.experimental import pallas as pl
from jax.experimental.pallas import tpu as pltpu
from jax.sharding import Mesh, PartitionSpec as P

ROWS_AXES = ("zh", "y", "c")
COLS_AXES = ("x", "zb", "za")
F32 = jnp.float32
BF16 = jnp.bfloat16


def copies(block, size):
    return jnp.broadcast_to(block[None], (size,) + block.shape)


def spread(block, axis, size):
    return lax.all_to_all(copies(block, size), axis, 0, 0, tiled=True)


def shifted(block, axis, size):
    return [block] + [
        lax.ppermute(block, axis, [(i, (i + n) % size) for i in range(size)])
        for n in range(1, size)
    ]


def swap(block, axis):
    return lax.ppermute(block, axis, [(0, 1), (1, 0)])


def fetch(place, pairs, weights, sems):
    matrices, hid, _ = weights.shape
    copies = [[] for _ in range(matrices)]
    row, part = 0, 0
    for pair in pairs:
        ny, height, depth = pair[0].shape
        start = 0
        while start < height:
            m, first = divmod(row, hid)
            count = min(hid - first, height - start)
            for k, ref in enumerate(pair):
                core = jnp.bitwise_xor(place[1], k)
                for y in range(ny):
                    at = pl.multiple_of((y * 2 + core) * depth, depth)
                    copy = pltpu.make_async_copy(
                        ref.at[y, pl.ds(start, count)],
                        weights.at[m, pl.ds(first, count), pl.ds(at, depth)],
                        sems.at[part, k * ny + y],
                    )
                    copy.start()
                    copies[m].append(copy)
            start, row, part = start + count, row + count, part + 1
    return copies


def near_kernel(
    place,
    acts_0, acts_1, acts_2, acts_3,
    own, core,
    part,
    tok_far,
    tok,
    weights,
    sems,
):
    acts = (acts_0, acts_1, acts_2, acts_3)
    nx = len(acts)
    na, nb, _, rows, width = acts_0.shape
    zh, me = place[0], place[2]
    copies = fetch(place, [(own, core)], weights, sems)

    for n in range(nx):
        x = lax.rem(me - n + nx, nx)
        base = lax.rem(x, nx // 2) * (nb * na)
        far = jnp.bitwise_xor(x // (nx // 2), zh)
        for a in range(na):
            for b in range(nb):
                zl = jnp.bitwise_xor(place[3], b) * na + a
                at = pl.multiple_of((base + zl) * width, width)
                for t in range(2):
                    tok[far, t, :, pl.ds(at, width)] = acts[n][a, b, t]
    tok_far[...] = tok[1]

    for m in range(3):
        for copy in copies[m]:
            copy.wait()
        part[m] = lax.dot_general(
            tok[0, m // 2], weights[m], (((1,), (1,)), ((), ())), preferred_element_type=F32
        )


def layer_kernel(
    place,
    part,
    tok_far,
    scale,
    near_own, near_core,
    first_own, first_core, last_own, last_core,
    outs,
    grad,
    near,
    far,
    sems,
):
    nx, nl, _, rows, width = outs.shape
    zh = place[0]
    far_copies = fetch(place, [(first_own, first_core), (last_own, last_core)], far, sems.at[1])
    near_copies = fetch(place, [(near_own, near_core)], near, sems.at[0])

    def times(t, m):
        for copy in far_copies[m]:
            copy.wait()
        return part[m] + lax.dot_general(
            tok_far[t], far[m], (((1,), (1,)), ((), ())), preferred_element_type=F32
        )

    gate_pre = times(0, 0)
    up_proj = times(0, 1)
    back = times(1, 2)
    sigmoid_gate = jax.nn.sigmoid(gate_pre)
    swish_gate = gate_pre * sigmoid_gate
    activated = swish_gate * up_proj
    hidden = (activated * scale[...]).astype(BF16)
    grad[...] = jnp.sum(back * activated, axis=0, keepdims=True)
    hidden_grad = back * scale[...]
    gate_grad = (
        hidden_grad * up_proj * sigmoid_gate * (1.0 + gate_pre * (1.0 - sigmoid_gate))
    ).astype(BF16)
    up_grad = (hidden_grad * swish_gate).astype(BF16)

    for m in range(3):
        for copy in near_copies[m]:
            copy.wait()
    for k, weights in enumerate((far, near)):
        half = jnp.bitwise_xor(zh, 1 - k)
        for n in range(nx * nl // 4):
            columns = slice(2 * n * width, 2 * (n + 1) * width)
            mixed = jnp.dot(hidden, weights[2, :, columns], preferred_element_type=F32)
            back_in = jnp.dot(
                gate_grad, weights[0, :, columns], preferred_element_type=F32
            ) + jnp.dot(up_grad, weights[1, :, columns], preferred_element_type=F32)
            for side in range(2):
                x, zl = divmod(2 * n + side, nl)
                x = half * (nx // 2) + x
                piece = slice(side * width, (side + 1) * width)
                outs[x, zl, 0] = mixed[:, piece].astype(BF16)
                outs[x, zl, 1] = back_in[:, piece].astype(BF16)


def whole():
    return pl.BlockSpec(memory_space=pltpu.VMEM)


def anywhere():
    return pl.BlockSpec(memory_space=pl.ANY)


def near_layer(place, acts, weights):
    nx = len(acts)
    na, nb, _, rows, width = acts[0].shape
    ny, height, _ = weights[0].shape
    hid = height // 3
    half = nx * na * nb * width // 2
    return pl.pallas_call(
        near_kernel,
        out_shape=(
            jax.ShapeDtypeStruct((3, rows, hid), F32),
            jax.ShapeDtypeStruct((2, rows, half), BF16),
        ),
        in_specs=[pl.BlockSpec(memory_space=pltpu.SMEM)] + [whole()] * len(acts) + [anywhere()] * 2,
        out_specs=(whole(), whole()),
        scratch_shapes=[
            pltpu.VMEM((2, 2, rows, half), BF16),
            pltpu.VMEM((3, hid, half), BF16),
            pltpu.SemaphoreType.DMA((3, 2 * ny)),
        ],
        compiler_params=pltpu.CompilerParams(vmem_limit_bytes=48 * 2**20),
        cost_estimate=pl.CostEstimate(
            flops=6 * rows * half * hid, bytes_accessed=6 * half * hid, transcendentals=0
        ),
    )(place, *acts, *weights)


def layer(place, part, tok_far, scale, weights, nx, nl):
    _, rows, half = tok_far.shape
    ny, height, _ = weights[0].shape
    hid = height // 3
    width = 2 * half // (nx * nl)
    return pl.pallas_call(
        layer_kernel,
        out_shape=(
            jax.ShapeDtypeStruct((nx, nl, 2, rows, width), BF16),
            jax.ShapeDtypeStruct((1, hid), F32),
        ),
        in_specs=[pl.BlockSpec(memory_space=pltpu.SMEM)] + [whole()] * 3 + [anywhere()] * 6,
        out_specs=(whole(), whole()),
        scratch_shapes=[
            pltpu.VMEM((3, hid, half), BF16),
            pltpu.VMEM((3, hid, half), BF16),
            pltpu.SemaphoreType.DMA((2, 4, 2 * ny)),
        ],
        compiler_params=pltpu.CompilerParams(vmem_limit_bytes=48 * 2**20),
        cost_estimate=pl.CostEstimate(
            flops=18 * rows * half * hid,
            bytes_accessed=12 * half * hid,
            transcendentals=rows * hid,
        ),
    )(place, part, tok_far, scale, *weights)


def total(blocks):
    wide = [block.astype(F32) for block in blocks]
    while len(wide) > 1:
        wide = [a + b for a, b in zip(wide[::2], wide[1::2])]
    return wide[0]


def make_per_device(size):
    ny, nx, nb, na = (size[a] for a in ("y", "x", "zb", "za"))

    def per_device(tokens, gate_weight, up_weight, down_weight, ia3_scale, cotangent):
        seq_len, seq_local, width = tokens.shape
        rows = seq_len * seq_local
        place = jnp.stack([lax.axis_index(a) for a in ("zh", "c", "x", "zb")])

        acts = jnp.stack([tokens.reshape(rows, width), cotangent.reshape(rows, width)])
        acts = spread(jnp.stack([acts, swap(acts, "zb")]), "za", na)

        mine = jnp.concatenate([gate_weight.T, up_weight.T, down_weight])
        cut = mine.shape[0] * 17 // 21
        near = copies(mine, ny)
        first, last = mine[:cut], mine[cut:]
        near, first, acts = lax.optimization_barrier((near, first, acts))
        first = swap(first, "zh")
        near_own = lax.all_to_all(near, "y", 0, 0, tiled=True)
        acts = shifted(acts, "x", nx)
        acts, near_own, first, last = lax.optimization_barrier((acts, near_own, first, last))

        last = swap(last, "zh")
        first_own = spread(first, "y", ny)
        near_core = swap(near_own, "c")
        part, tok_far = near_layer(place, acts, (near_own, near_core))
        first_own, last, part = lax.optimization_barrier((first_own, last, part))

        first_core = swap(first_own, "c")
        last_own = spread(last, "y", ny)
        last_core = swap(last_own, "c")
        weights = (near_own, near_core, first_own, first_core, last_own, last_core)
        outs, grad = layer(place, part, tok_far, ia3_scale.reshape(1, -1), weights, nx, nb * na)

        grad = grad + swap(grad, "zh")
        grad = grad + swap(grad, "c")
        outs = lax.all_to_all(outs, "x", 0, 0, tiled=True)
        outs = total([outs[i] for i in range(nx)]).astype(BF16)
        outs, grad = lax.optimization_barrier((outs, grad))
        scale_grad = total(shifted(grad, "y", ny)).reshape(-1)
        outs = outs.reshape((nb, na) + outs.shape[1:]).swapaxes(0, 1)
        outs = lax.all_to_all(outs, "za", 0, 0, tiled=True)
        outs = total([outs[i] for i in range(na)])
        mine, theirs = [
            lax.dynamic_index_in_dim(outs, jnp.bitwise_xor(place[3], k), 0, False) for k in range(2)
        ]
        outs = (mine + swap(theirs.astype(BF16), "zb").astype(F32)).astype(BF16)
        return outs[0].reshape(tokens.shape), outs[1].reshape(tokens.shape), scale_grad

    return per_device


def solution(mesh):
    shape = {"zh": 2, "y": 4, "c": 2, "x": 4, "zb": 2, "za": 4}
    fine = Mesh(mesh.devices.reshape(tuple(shape.values())), tuple(shape))
    in_specs = (
        P(None, ROWS_AXES, COLS_AXES),
        P(ROWS_AXES, COLS_AXES),
        P(ROWS_AXES, COLS_AXES),
        P(COLS_AXES, ROWS_AXES),
        P(COLS_AXES),
        P(None, ROWS_AXES, COLS_AXES),
    )
    out_specs = (
        P(None, ROWS_AXES, COLS_AXES),
        P(None, ROWS_AXES, COLS_AXES),
        P(COLS_AXES),
    )
    return jax.shard_map(
        make_per_device(shape),
        mesh=fine,
        in_specs=in_specs,
        out_specs=out_specs,
        check_vma=False,
    )
```

```python
import jax
import jax.numpy as jnp
from jax import lax
from jax.experimental import pallas as pl
from jax.experimental.pallas import tpu as pltpu
from jax.sharding import Mesh, PartitionSpec as P

ROWS_AXES = ("zh", "y", "c")
COLS_AXES = ("x", "zb", "za")
F32 = jnp.float32
BF16 = jnp.bfloat16


def copies(block, size):
    return jnp.broadcast_to(block[None], (size,) + block.shape)


def spread(block, axis, size):
    return lax.all_to_all(copies(block, size), axis, 0, 0, tiled=True)


def shifted(block, axis, size):
    return [block] + [
        lax.ppermute(block, axis, [(i, (i + n) % size) for i in range(size)])
        for n in range(1, size)
    ]


def swap(block, axis):
    return lax.ppermute(block, axis, [(0, 1), (1, 0)])


def fetch(place, pairs, weights, sems):
    matrices, hid, _ = weights.shape
    copies = [[] for _ in range(matrices)]
    row, part = 0, 0
    for pair in pairs:
        ny, height, depth = pair[0].shape
        start = 0
        while start < height:
            m, first = divmod(row, hid)
            count = min(hid - first, height - start)
            for k, ref in enumerate(pair):
                core = jnp.bitwise_xor(place[1], k)
                for y in range(ny):
                    at = pl.multiple_of((y * 2 + core) * depth, depth)
                    copy = pltpu.make_async_copy(
                        ref.at[y, pl.ds(start, count)],
                        weights.at[m, pl.ds(first, count), pl.ds(at, depth)],
                        sems.at[part, k * ny + y],
                    )
                    copy.start()
                    copies[m].append(copy)
            start, row, part = start + count, row + count, part + 1
    return copies


def near_kernel(
    place,
    acts_0, acts_1, acts_2, acts_3,
    own, core,
    part,
    tok_far,
    tok,
    weights,
    sems,
):
    acts = (acts_0, acts_1, acts_2, acts_3)
    nx = len(acts)
    na, nb, _, rows, width = acts_0.shape
    zh, me = place[0], place[2]
    copies = fetch(place, [(own, core)], weights, sems)

    for n in range(nx):
        x = lax.rem(me - n + nx, nx)
        base = lax.rem(x, nx // 2) * (nb * na)
        far = jnp.bitwise_xor(x // (nx // 2), zh)
        for a in range(na):
            for b in range(nb):
                zl = jnp.bitwise_xor(place[3], b) * na + a
                at = pl.multiple_of((base + zl) * width, width)
                for t in range(2):
                    tok[far, t, :, pl.ds(at, width)] = acts[n][a, b, t]
    tok_far[...] = tok[1]

    for m in range(3):
        for copy in copies[m]:
            copy.wait()
        part[m] = lax.dot_general(
            tok[0, m // 2], weights[m], (((1,), (1,)), ((), ())), preferred_element_type=F32
        )


def layer_kernel(
    place,
    part,
    tok_far,
    scale,
    near_own, near_core,
    first_own, first_core, last_own, last_core,
    outs,
    grad,
    near,
    far,
    sems,
):
    nx, na, nb, _, rows, width = outs.shape
    nl = nb * na
    zh = place[0]
    far_copies = fetch(place, [(first_own, first_core), (last_own, last_core)], far, sems.at[1])
    near_copies = fetch(place, [(near_own, near_core)], near, sems.at[0])

    def times(t, m):
        for copy in far_copies[m]:
            copy.wait()
        return part[m] + lax.dot_general(
            tok_far[t], far[m], (((1,), (1,)), ((), ())), preferred_element_type=F32
        )

    gate_pre = times(0, 0)
    up_proj = times(0, 1)
    back = times(1, 2)
    sigmoid_gate = jax.nn.sigmoid(gate_pre)
    swish_gate = gate_pre * sigmoid_gate
    activated = swish_gate * up_proj
    hidden = (activated * scale[...]).astype(BF16)
    grad[...] = jnp.sum(back * activated, axis=0, keepdims=True)
    hidden_grad = back * scale[...]
    gate_grad = (
        hidden_grad * up_proj * sigmoid_gate * (1.0 + gate_pre * (1.0 - sigmoid_gate))
    ).astype(BF16)
    up_grad = (hidden_grad * swish_gate).astype(BF16)

    for m in range(3):
        for copy in near_copies[m]:
            copy.wait()
    for k, weights in enumerate((far, near)):
        half = jnp.bitwise_xor(zh, 1 - k)
        for n in range(nx * nl // 4):
            columns = slice(2 * n * width, 2 * (n + 1) * width)
            mixed = jnp.dot(hidden, weights[2, :, columns], preferred_element_type=F32)
            back_in = jnp.dot(
                gate_grad, weights[0, :, columns], preferred_element_type=F32
            ) + jnp.dot(up_grad, weights[1, :, columns], preferred_element_type=F32)
            for side in range(2):
                x, zl = divmod(2 * n + side, nl)
                x = half * (nx // 2) + x
                piece = slice(side * width, (side + 1) * width)
                outs[x, zl % na, zl // na, 0] = mixed[:, piece].astype(BF16)
                outs[x, zl % na, zl // na, 1] = back_in[:, piece].astype(BF16)


def whole():
    return pl.BlockSpec(memory_space=pltpu.VMEM)


def anywhere():
    return pl.BlockSpec(memory_space=pl.ANY)


def near_layer(place, acts, weights):
    nx = len(acts)
    na, nb, _, rows, width = acts[0].shape
    ny, height, _ = weights[0].shape
    hid = height // 3
    half = nx * na * nb * width // 2
    return pl.pallas_call(
        near_kernel,
        out_shape=(
            jax.ShapeDtypeStruct((3, rows, hid), F32),
            jax.ShapeDtypeStruct((2, rows, half), BF16),
        ),
        in_specs=[pl.BlockSpec(memory_space=pltpu.SMEM)] + [whole()] * len(acts) + [anywhere()] * 2,
        out_specs=(whole(), whole()),
        scratch_shapes=[
            pltpu.VMEM((2, 2, rows, half), BF16),
            pltpu.VMEM((3, hid, half), BF16),
            pltpu.SemaphoreType.DMA((3, 2 * ny)),
        ],
        compiler_params=pltpu.CompilerParams(vmem_limit_bytes=48 * 2**20),
        cost_estimate=pl.CostEstimate(
            flops=6 * rows * half * hid, bytes_accessed=6 * half * hid, transcendentals=0
        ),
    )(place, *acts, *weights)


def layer(place, part, tok_far, scale, weights, nx, nb, na):
    _, rows, half = tok_far.shape
    ny, height, _ = weights[0].shape
    hid = height // 3
    width = 2 * half // (nx * nb * na)
    return pl.pallas_call(
        layer_kernel,
        out_shape=(
            jax.ShapeDtypeStruct((nx, na, nb, 2, rows, width), BF16),
            jax.ShapeDtypeStruct((1, hid), F32),
        ),
        in_specs=[pl.BlockSpec(memory_space=pltpu.SMEM)] + [whole()] * 3 + [anywhere()] * 6,
        out_specs=(whole(), whole()),
        scratch_shapes=[
            pltpu.VMEM((3, hid, half), BF16),
            pltpu.VMEM((3, hid, half), BF16),
            pltpu.SemaphoreType.DMA((2, 4, 2 * ny)),
        ],
        compiler_params=pltpu.CompilerParams(vmem_limit_bytes=48 * 2**20),
        cost_estimate=pl.CostEstimate(
            flops=18 * rows * half * hid,
            bytes_accessed=12 * half * hid,
            transcendentals=rows * hid,
        ),
    )(place, part, tok_far, scale, *weights)


def total(blocks):
    wide = [block.astype(F32) for block in blocks]
    while len(wide) > 1:
        wide = [a + b for a, b in zip(wide[::2], wide[1::2])]
    return wide[0]


def make_per_device(size):
    ny, nx, nb, na = (size[a] for a in ("y", "x", "zb", "za"))

    def per_device(tokens, gate_weight, up_weight, down_weight, ia3_scale, cotangent):
        seq_len, seq_local, width = tokens.shape
        rows = seq_len * seq_local
        place = jnp.stack([lax.axis_index(a) for a in ("zh", "c", "x", "zb")])

        acts = jnp.stack([tokens.reshape(rows, width), cotangent.reshape(rows, width)])
        mine = jnp.concatenate([gate_weight.T, up_weight.T, down_weight])
        cut = mine.shape[0] * 17 // 21
        near = copies(mine, ny)
        first, last = mine[:cut], mine[cut:]
        acts = jnp.stack([acts, swap(acts, "zb")])
        acts, near, first = lax.optimization_barrier((acts, near, first))
        acts = spread(acts, "za", na)

        near, first, acts = lax.optimization_barrier((near, first, acts))
        first = swap(first, "zh")
        near_own = lax.all_to_all(near, "y", 0, 0, tiled=True)
        acts = shifted(acts, "x", nx)
        acts, near_own, first, last = lax.optimization_barrier((acts, near_own, first, last))

        last = swap(last, "zh")
        first_own = spread(first, "y", ny)
        near_core = swap(near_own, "c")
        part, tok_far = near_layer(place, acts, (near_own, near_core))
        first_own, last, part = lax.optimization_barrier((first_own, last, part))

        first_core = swap(first_own, "c")
        last_own = spread(last, "y", ny)
        last_own, first_core = lax.optimization_barrier((last_own, first_core))
        last_core = swap(last_own, "c")
        weights = (near_own, near_core, first_own, first_core, last_own, last_core)
        outs, grad = layer(place, part, tok_far, ia3_scale.reshape(1, -1), weights, nx, nb, na)

        grad = grad + swap(grad, "zh")
        grad = grad + swap(grad, "c")
        outs = lax.all_to_all(outs, "x", 0, 0, tiled=True)
        outs = total([outs[i] for i in range(nx)]).astype(BF16)
        outs, grad = lax.optimization_barrier((outs, grad))
        scale_grad = total(shifted(grad, "y", ny)).reshape(-1)
        outs = lax.all_to_all(outs, "za", 0, 0, tiled=True)
        outs = total([outs[i] for i in range(na)])
        mine, theirs = [
            lax.dynamic_index_in_dim(outs, jnp.bitwise_xor(place[3], k), 0, False) for k in range(2)
        ]
        outs = (mine + swap(theirs.astype(BF16), "zb").astype(F32)).astype(BF16)
        return outs[0].reshape(tokens.shape), outs[1].reshape(tokens.shape), scale_grad

    return per_device


def solution(mesh):
    shape = {"zh": 2, "y": 4, "c": 2, "x": 4, "zb": 2, "za": 4}
    fine = Mesh(mesh.devices.reshape(tuple(shape.values())), tuple(shape))
    in_specs = (
        P(None, ROWS_AXES, COLS_AXES),
        P(ROWS_AXES, COLS_AXES),
        P(ROWS_AXES, COLS_AXES),
        P(COLS_AXES, ROWS_AXES),
        P(COLS_AXES),
        P(None, ROWS_AXES, COLS_AXES),
    )
    out_specs = (
        P(None, ROWS_AXES, COLS_AXES),
        P(None, ROWS_AXES, COLS_AXES),
        P(COLS_AXES),
    )
    return jax.shard_map(
        make_per_device(shape),
        mesh=fine,
        in_specs=in_specs,
        out_specs=out_specs,
        check_vma=False,
    )
```

```python
import jax
import jax.numpy as jnp
from jax import lax
from jax.experimental import pallas as pl
from jax.experimental.pallas import tpu as pltpu
from jax.sharding import Mesh, PartitionSpec as P

ROWS_AXES = ("zh", "y", "c")
COLS_AXES = ("x", "zb", "za")
F32 = jnp.float32
BF16 = jnp.bfloat16


def copies(block, size):
    return jnp.broadcast_to(block[None], (size,) + block.shape)


def spread(block, axis, size):
    return lax.all_to_all(copies(block, size), axis, 0, 0, tiled=True)


def shifted(block, axis, size):
    return [block] + [
        lax.ppermute(block, axis, [(i, (i + n) % size) for i in range(size)])
        for n in range(1, size)
    ]


def swap(block, axis):
    return lax.ppermute(block, axis, [(0, 1), (1, 0)])


def fetch(place, pairs, weights, sems):
    matrices, hid, _ = weights.shape
    copies = [[] for _ in range(matrices)]
    row, part = 0, 0
    for pair in pairs:
        ny, height, depth = pair[0].shape
        start = 0
        while start < height:
            m, first = divmod(row, hid)
            count = min(hid - first, height - start)
            for k, ref in enumerate(pair):
                core = jnp.bitwise_xor(place[1], k)
                for y in range(ny):
                    block = y if len(pair) == 1 else y * 2 + core
                    at = pl.multiple_of(block * depth, depth)
                    copy = pltpu.make_async_copy(
                        ref.at[y, pl.ds(start, count)],
                        weights.at[m, pl.ds(first, count), pl.ds(at, depth)],
                        sems.at[part, k * ny + y],
                    )
                    copy.start()
                    copies[m].append(copy)
            start, row, part = start + count, row + count, part + 1
    return copies


def near_kernel(
    place,
    acts_0, acts_1, acts_2, acts_3,
    own, core,
    part,
    tok_far,
    tok,
    weights,
    sems,
):
    acts = (acts_0, acts_1, acts_2, acts_3)
    nx = len(acts)
    na, nb, _, rows, width = acts_0.shape
    zh, me = place[0], place[2]
    copies = fetch(place, [(own, core)], weights, sems)

    for n in range(nx):
        x = lax.rem(me - n + nx, nx)
        base = lax.rem(x, nx // 2) * (nb * na)
        far = jnp.bitwise_xor(x // (nx // 2), zh)
        for a in range(na):
            for b in range(nb):
                zl = jnp.bitwise_xor(place[3], b) * na + a
                at = pl.multiple_of((base + zl) * width, width)
                for t in range(2):
                    tok[far, t, :, pl.ds(at, width)] = acts[n][a, b, t]
    tok_far[...] = tok[1]

    for m in range(3):
        for copy in copies[m]:
            copy.wait()
        part[m] = lax.dot_general(
            tok[0, m // 2], weights[m], (((1,), (1,)), ((), ())), preferred_element_type=F32
        )


def layer_kernel(
    place,
    part,
    tok_far,
    scale,
    near_own, near_core,
    first_own, first_core,
    last,
    outs,
    grad,
    near,
    far,
    sems,
):
    nx, na, nb, _, rows, width = outs.shape
    nl = nb * na
    zh = place[0]
    far_copies = fetch(place, [(first_own, first_core), (last,)], far, sems.at[1])
    near_copies = fetch(place, [(near_own, near_core)], near, sems.at[0])

    def times(t, m):
        for copy in far_copies[m]:
            copy.wait()
        return part[m] + lax.dot_general(
            tok_far[t], far[m], (((1,), (1,)), ((), ())), preferred_element_type=F32
        )

    gate_pre = times(0, 0)
    up_proj = times(0, 1)
    back = times(1, 2)
    sigmoid_gate = jax.nn.sigmoid(gate_pre)
    swish_gate = gate_pre * sigmoid_gate
    activated = swish_gate * up_proj
    hidden = (activated * scale[...]).astype(BF16)
    grad[...] = jnp.sum(back * activated, axis=0, keepdims=True)
    hidden_grad = back * scale[...]
    gate_grad = (
        hidden_grad * up_proj * sigmoid_gate * (1.0 + gate_pre * (1.0 - sigmoid_gate))
    ).astype(BF16)
    up_grad = (hidden_grad * swish_gate).astype(BF16)

    for m in range(3):
        for copy in near_copies[m]:
            copy.wait()
    for k, weights in enumerate((far, near)):
        half = jnp.bitwise_xor(zh, 1 - k)
        for n in range(nx * nl // 4):
            columns = slice(2 * n * width, 2 * (n + 1) * width)
            mixed = jnp.dot(hidden, weights[2, :, columns], preferred_element_type=F32)
            back_in = jnp.dot(
                gate_grad, weights[0, :, columns], preferred_element_type=F32
            ) + jnp.dot(up_grad, weights[1, :, columns], preferred_element_type=F32)
            for side in range(2):
                x, zl = divmod(2 * n + side, nl)
                x = half * (nx // 2) + x
                piece = slice(side * width, (side + 1) * width)
                outs[x, zl % na, zl // na, 0] = mixed[:, piece].astype(BF16)
                outs[x, zl % na, zl // na, 1] = back_in[:, piece].astype(BF16)


def whole():
    return pl.BlockSpec(memory_space=pltpu.VMEM)


def anywhere():
    return pl.BlockSpec(memory_space=pl.ANY)


def near_layer(place, acts, weights):
    nx = len(acts)
    na, nb, _, rows, width = acts[0].shape
    ny, height, _ = weights[0].shape
    hid = height // 3
    half = nx * na * nb * width // 2
    return pl.pallas_call(
        near_kernel,
        out_shape=(
            jax.ShapeDtypeStruct((3, rows, hid), F32),
            jax.ShapeDtypeStruct((2, rows, half), BF16),
        ),
        in_specs=[pl.BlockSpec(memory_space=pltpu.SMEM)] + [whole()] * len(acts) + [anywhere()] * 2,
        out_specs=(whole(), whole()),
        scratch_shapes=[
            pltpu.VMEM((2, 2, rows, half), BF16),
            pltpu.VMEM((3, hid, half), BF16),
            pltpu.SemaphoreType.DMA((3, 2 * ny)),
        ],
        compiler_params=pltpu.CompilerParams(vmem_limit_bytes=48 * 2**20),
        cost_estimate=pl.CostEstimate(
            flops=6 * rows * half * hid, bytes_accessed=6 * half * hid, transcendentals=0
        ),
    )(place, *acts, *weights)


def layer(place, part, tok_far, scale, weights, nx, nb, na):
    _, rows, half = tok_far.shape
    ny, height, _ = weights[0].shape
    hid = height // 3
    width = 2 * half // (nx * nb * na)
    return pl.pallas_call(
        layer_kernel,
        out_shape=(
            jax.ShapeDtypeStruct((nx, na, nb, 2, rows, width), BF16),
            jax.ShapeDtypeStruct((1, hid), F32),
        ),
        in_specs=[pl.BlockSpec(memory_space=pltpu.SMEM)] + [whole()] * 3 + [anywhere()] * 5,
        out_specs=(whole(), whole()),
        scratch_shapes=[
            pltpu.VMEM((3, hid, half), BF16),
            pltpu.VMEM((3, hid, half), BF16),
            pltpu.SemaphoreType.DMA((2, 4, 2 * ny)),
        ],
        compiler_params=pltpu.CompilerParams(vmem_limit_bytes=48 * 2**20),
        cost_estimate=pl.CostEstimate(
            flops=18 * rows * half * hid,
            bytes_accessed=12 * half * hid,
            transcendentals=rows * hid,
        ),
    )(place, part, tok_far, scale, *weights)


def total(blocks):
    wide = [block.astype(F32) for block in blocks]
    while len(wide) > 1:
        wide = [a + b for a, b in zip(wide[::2], wide[1::2])]
    return wide[0]


def make_per_device(size):
    ny, nx, nb, na = (size[a] for a in ("y", "x", "zb", "za"))

    def per_device(tokens, gate_weight, up_weight, down_weight, ia3_scale, cotangent):
        seq_len, seq_local, width = tokens.shape
        rows = seq_len * seq_local
        place = jnp.stack([lax.axis_index(a) for a in ("zh", "c", "x", "zb")])

        acts = jnp.stack([tokens.reshape(rows, width), cotangent.reshape(rows, width)])
        mine = jnp.concatenate([gate_weight.T, up_weight.T, down_weight])
        cut = mine.shape[0] * 17 // 21
        near = copies(mine, ny)
        first, last = mine[:cut], mine[cut:]
        acts = jnp.stack([acts, swap(acts, "zb")])
        acts, near, first = lax.optimization_barrier((acts, near, first))
        acts = spread(acts, "za", na)

        near, first, acts = lax.optimization_barrier((near, first, acts))
        first = swap(first, "zh")
        near_own = lax.all_to_all(near, "y", 0, 0, tiled=True)
        acts = shifted(acts, "x", nx)
        acts, near_own, first, last = lax.optimization_barrier((acts, near_own, first, last))

        last = swap(last, "zh")
        first_own = spread(first, "y", ny)
        near_core = swap(near_own, "c")
        part, tok_far = near_layer(place, acts, (near_own, near_core))
        first_own, last, part = lax.optimization_barrier((first_own, last, part))

        first_core = swap(first_own, "c")
        last = spread(last, ("y", "c"), 2 * ny)
        weights = (near_own, near_core, first_own, first_core, last)
        outs, grad = layer(place, part, tok_far, ia3_scale.reshape(1, -1), weights, nx, nb, na)

        grad = grad + swap(grad, "zh")
        grad = grad + swap(grad, "c")
        outs = lax.all_to_all(outs, "x", 0, 0, tiled=True)
        outs = total([outs[i] for i in range(nx)]).astype(BF16)
        outs, grad = lax.optimization_barrier((outs, grad))
        scale_grad = total(shifted(grad, "y", ny)).reshape(-1)
        outs = lax.all_to_all(outs, "za", 0, 0, tiled=True)
        outs = total([outs[i] for i in range(na)])
        mine, theirs = [
            lax.dynamic_index_in_dim(outs, jnp.bitwise_xor(place[3], k), 0, False) for k in range(2)
        ]
        outs = (mine + swap(theirs.astype(BF16), "zb").astype(F32)).astype(BF16)
        return outs[0].reshape(tokens.shape), outs[1].reshape(tokens.shape), scale_grad

    return per_device


def solution(mesh):
    shape = {"zh": 2, "y": 4, "c": 2, "x": 4, "zb": 2, "za": 4}
    fine = Mesh(mesh.devices.reshape(tuple(shape.values())), tuple(shape))
    in_specs = (
        P(None, ROWS_AXES, COLS_AXES),
        P(ROWS_AXES, COLS_AXES),
        P(ROWS_AXES, COLS_AXES),
        P(COLS_AXES, ROWS_AXES),
        P(COLS_AXES),
        P(None, ROWS_AXES, COLS_AXES),
    )
    out_specs = (
        P(None, ROWS_AXES, COLS_AXES),
        P(None, ROWS_AXES, COLS_AXES),
        P(COLS_AXES),
    )
    return jax.shard_map(
        make_per_device(shape),
        mesh=fine,
        in_specs=in_specs,
        out_specs=out_specs,
        check_vma=False,
    )
```
